32 devices in a mesh: sec: 2 (over core), blk: 16 (over z, y, x).
Axes of the slice: x: 2, y: 2, z: 4, core: 2. Of those that a mesh axis runs over, the one named last changes fastest.
Arguments:
- state: float32 [2, 32, 40, 16384], P('sec', None, None, 'blk'), may hold values from -6 to 6
- diffusion: float32 [2, 40, 16384], P('sec', None, 'blk'), may hold values from 0.05 to 0.25
- transport: float32 [2, 40, 16384], P('sec', None, 'blk'), may hold values from 0.1 to 0.4
- mixing: float32 [2, 40, 40], P('sec'), may hold values from -1 to 1
- src_col: int32 [2, 16, 16, 128], P('sec', 'blk'), may hold values from 0 to 1023
- weights: float32 [2, 16, 16, 128], P('sec', 'blk'), may hold values from 0.05 to 0.25
- counts: int32 [2, 16, 16], P('sec', 'blk'), may hold values from 8 to 128, as said below
- recv_rows: int32 [2, 16, 16, 128], P('sec', 'blk'), may hold values from 0 to 1023
Outputs:
- new_state: float32 [2, 32, 40, 16384], P('sec', None, None, 'blk')
- incoming: float32 [2, 32, 16384], P('sec', None, 'blk')
The draws below stay inside these ranges and needn't reach their ends.
Inputs may be any that keep to these rules, and one draw needn't show every extreme that they name: `counts`: for each sending component, one destination block drawn from the seed has all 128 slots live from every source block.
All inputs are finite; a program needn't handle non-finite values.
Results may differ from the reference program's by a relative error of at most 0.0003.
Values sent between devices are 32-bit elements; how exact they have to be, the bound alone decides.
A program may use at most 64 MiB of HBM per device.

```python
import jax
import jax.numpy as jnp
from jax import lax

VARS = 32
LEV = 40
SUBSTEPS = 2
CELL_DEV = 1024
P_SIZE = 128
BLOCKS = 16
CELLS = 16384


def draw_counts(key, part):
    key = jax.random.fold_in(key, 7)
    first_key, second_key = jax.random.split(key)
    ragged = jax.random.randint(first_key, (2, BLOCKS, BLOCKS), max(1, P_SIZE // 16), P_SIZE + 1)
    chosen = jax.random.randint(second_key, (2,), 0, BLOCKS)
    marked = jnp.arange(BLOCKS)[None, None, :] == chosen[:, None, None]
    return jnp.where(marked, P_SIZE, ragged).astype(jnp.int32)


def set_ends(result, own_key, low, high):
    shape = result.shape
    spot = [jax.random.randint(jax.random.fold_in(own_key, axis), (), 0, shape[axis]) for axis in range(len(shape))]
    result = result.at[tuple(spot)].set(low)
    longest = shape.index(max(shape))
    spot[longest] = (spot[longest] + 1) % shape[longest]
    return result.at[tuple(spot)].set(high)


def shard_levels(own_key, extent, pieces, least, high):
    gain = 1.0
    for position, parts in pieces:
        steps = jax.random.uniform(jax.random.fold_in(jax.random.fold_in(own_key, 6), position), (parts,), jnp.float32, least / len(pieces), high / len(pieces))
        gain = gain * jnp.repeat(jnp.exp(steps), extent[position] // parts).reshape((-1,) + (1,) * (len(extent) - 1 - position))
    return gain


def bell_draw(stream_key, extent, width, bound, shards=(), held_as=jnp.bfloat16):
    result = jax.random.normal(stream_key, extent, jnp.float32) * width
    if len(shards) > 0:
        result = shard_levels(stream_key, extent, shards, -0.22, 0.18) * result
    return jnp.clip(result, min=-bound, max=bound).astype(held_as)


def setup_inputs(seed: int = 0) -> dict:
    key_list = jax.random.split(jax.random.key(seed), 9)
    return {
        "state": bell_draw(key_list[0], (2, VARS, LEV, CELLS), 1.0, 6.0, ((0, 2), (3, 16)), jnp.float32),
        "diffusion": jnp.clip(0.05 + 0.2 * jax.random.uniform(key_list[1], (2, LEV, CELLS), jnp.float32) ** shard_levels(key_list[1], (2, LEV, CELLS), ((0, 2), (2, 16)), -0.2, 0.2), 0.05, 0.25),
        "transport": jnp.clip(0.1 + 0.3 * jax.random.uniform(key_list[2], (2, LEV, CELLS), jnp.float32) ** shard_levels(key_list[2], (2, LEV, CELLS), ((0, 2), (2, 16)), -0.2, 0.2), 0.1, 0.4),
        "mixing": bell_draw(key_list[3], (2, LEV, LEV), LEV ** -0.5, 1.0, ((0, 2),), jnp.float32),
        "src_col": set_ends(jax.random.randint(key_list[4], (2, BLOCKS, BLOCKS, P_SIZE), 0, CELL_DEV), jax.random.fold_in(key_list[4], 1), 0, CELL_DEV - 1).astype(jnp.int32),
        "weights": jnp.clip(0.05 + 0.2 * jax.random.uniform(key_list[5], (2, BLOCKS, BLOCKS, P_SIZE), jnp.float32) ** shard_levels(key_list[5], (2, BLOCKS, BLOCKS, P_SIZE), ((0, 2), (1, 16)), -0.2, 0.2), 0.05, 0.25),
        "counts": draw_counts(jax.random.fold_in(key_list[8], 71), 0),
        "recv_rows": set_ends(jax.random.randint(key_list[7], (2, BLOCKS, BLOCKS, P_SIZE), 0, CELL_DEV), jax.random.fold_in(key_list[7], 1), 0, CELL_DEV - 1).astype(jnp.int32),
    }


def advance(field, rate_diff, rate_flow):
    left = jnp.roll(field, 1, axis=-1)
    right = jnp.roll(field, -1, axis=-1)
    return field + rate_diff * (left - 2.0 * field + right) + rate_flow * (left - field)


def reference(state, diffusion, transport, mixing, src_col, weights, counts, recv_rows):
    moved = state
    for step in range(SUBSTEPS):
        moved = advance(moved, diffusion[:, None], transport[:, None])
    column = moved + jnp.einsum("sij,svjc->svic", mixing, moved, precision=lax.Precision.HIGHEST)
    surface = column[:, :, 0, :]
    block_base = (jnp.arange(BLOCKS, dtype=jnp.int32) * CELL_DEV)[:, None, None]
    slot_index = jnp.arange(P_SIZE, dtype=jnp.int32)[None, None, :]
    results = []
    for target in range(2):
        sender = 1 - target
        global_col = block_base + src_col[sender]
        active_mask = slot_index < counts[sender][:, :, None]
        picked = surface[sender][:, global_col]
        values = jnp.where(active_mask[None], weights[sender][None] * picked, jnp.float32(0.0))
        global_row = jnp.transpose(block_base + recv_rows[target], (1, 0, 2))
        summed = jax.ops.segment_sum(values.reshape(VARS, -1).T, global_row.reshape(-1), CELLS)
        results.append(summed.T)
    incoming = jnp.stack(results)
    top = surface + 0.5 * (incoming - surface)
    new_state = column.at[:, :, 0, :].set(top)
    return new_state, incoming
```

```python
import functools

import jax
import jax.numpy as jnp
from jax import lax
from jax.experimental import pallas as pl
from jax.experimental.pallas import tpu as pltpu
from jax.sharding import PartitionSpec as P

MESH = pl.DeviceIdType.MESH
F32 = jnp.float32
BF16 = jnp.bfloat16
GROUP = 2
CHUNKS = 4
LANES = 128
SELECTOR_BYTES = 8 << 20


def lanes_of(shape):
    return lax.broadcasted_iota(jnp.int32, shape, len(shape) - 1)


def rows_of(shape):
    return lax.broadcasted_iota(jnp.int32, shape, len(shape) - 2)


def column_of(row, count):
    shape = (count, row.shape[1])
    spread = jnp.where(lanes_of(shape) == rows_of(shape), jnp.broadcast_to(row, shape), 0.0)
    return jnp.sum(spread, axis=1, keepdims=True)


def pieces_of(values):
    high = values.astype(BF16)
    low = (values - high.astype(F32)).astype(BF16)
    return jnp.concatenate([high, low], axis=0)


def kernel(
    nblocks, prebuilt,
    state, diffusion, transport, mixing, src_col, weights, counts, recv_rows,
    out, incoming,
    u, dif, tra, mix, src, wgt, cnt, rec,
    rate_a, rate_b, rate_d, edge_l, edge_r, msg_l, msg_r, from_l, from_r,
    surf, sendbuf, recvbuf, total, picker, placer,
    chunk_sem, small_sem, halo_send, halo_recv, send_sem, recv_sem,
):
    nvar, nlev, ncell = u.shape
    nslot = src.shape[1]
    ngroup = nblocks // GROUP
    sec = lax.axis_index("sec")
    blk = lax.axis_index("blk")
    other = 1 - sec
    left = lax.rem(blk + nblocks - 1, nblocks)
    right = lax.rem(blk + 1, nblocks)
    barrier = pltpu.get_barrier_semaphore()

    @pl.loop(0, nblocks)
    def greet(k):
        pl.semaphore_signal(barrier, inc=1, device_id=(other, lax.rem(blk + k, nblocks)), device_id_type=MESH)

    for side in (left, right):
        pl.semaphore_signal(barrier, inc=1, device_id=(sec, side), device_id_type=MESH)

    small = [
        pltpu.make_async_copy(source, target, small_sem.at[i])
        for i, (source, target) in enumerate(
            (
                (src_col.at[0, 0], src),
                (diffusion.at[0], dif),
                (transport.at[0], tra),
                (mixing.at[0], mix),
                (weights.at[0, 0], wgt),
                (counts.at[0], cnt),
                (recv_rows.at[0, 0], rec),
            )
        )
    ]
    for copy in small:
        copy.start()
    per_chunk = nvar // CHUNKS
    chunks = [
        pltpu.make_async_copy(
            state.at[0, pl.ds(i * per_chunk, per_chunk)],
            u.at[pl.ds(i * per_chunk, per_chunk)],
            chunk_sem.at[i],
        )
        for i in range(CHUNKS)
    ]
    for copy in chunks:
        copy.start()
    for copy in small:
        copy.wait()

    def selector(index_ref, base):
        parts = []
        for g in range(GROUP):
            row = index_ref[pl.ds(base + g, 1), :]
            cells = rows_of((ncell, nslot))
            parts.append(jnp.where(cells == jnp.broadcast_to(row, (ncell, nslot)), 1.0, 0.0).astype(BF16))
        return jnp.concatenate(parts, axis=1)

    cell = lanes_of((nlev, ncell))
    d_all = dif[...]
    b_all = d_all + tra[...]
    rate_a[...] = 1.0 - d_all - b_all
    rate_b[...] = jnp.where(cell == 0, 0.0, b_all)
    rate_d[...] = jnp.where(cell == ncell - 1, 0.0, d_all)
    d_first, d_last = dif[:, :LANES], dif[:, ncell - LANES :]
    b_first = d_first + tra[:, :LANES]
    b_last = d_last + tra[:, ncell - LANES :]
    a_first, a_last = 1.0 - d_first - b_first, 1.0 - d_last - b_last
    a0, b0, b1, d0 = a_first[:, 0:1], b_first[:, 0:1], b_first[:, 1:2], d_first[:, 0:1]
    an, bn = a_last[:, LANES - 1 :], b_last[:, LANES - 1 :]
    dn, dm = d_last[:, LANES - 1 :], d_last[:, LANES - 2 : LANES - 1]

    if prebuilt:

        @pl.loop(0, ngroup)
        def build_picker(g):
            picker[g] = selector(src, g * GROUP)

    live = lanes_of(wgt.shape).astype(F32) < column_of(cnt[...].astype(F32), nblocks)
    wgt[...] = jnp.where(live, wgt[...], 0.0)

    lane = lanes_of((nlev, LANES))
    even = lax.rem(lane, 2) == 0
    edge_l[...] = jnp.zeros_like(edge_l)
    edge_r[...] = jnp.zeros_like(edge_r)
    for i in range(CHUNKS):
        chunks[i].wait()

        @pl.loop(i * per_chunk, (i + 1) * per_chunk)
        def pack(v):
            mine = lax.div(lane, 2) == v
            first = pltpu.roll(u[v, :, 0:LANES], 2 * v, 1)
            last = pltpu.roll(u[v, :, ncell - LANES : ncell], 2 * v + 2, 1)
            edge_l[...] = jnp.where(mine, first, edge_l[...])
            edge_r[...] = jnp.where(mine, last, edge_r[...])

    el, er = edge_l[...], edge_r[...]
    after = lambda x: pltpu.roll(x, LANES - 1, 1)
    before = lambda x: pltpu.roll(x, 1, 1)
    is_rate = lane == 2 * nvar
    msg_r[...] = jnp.where(is_rate, dn, jnp.where(even, after(er), an * er + bn * before(er)))
    msg_l[...] = jnp.where(is_rate, b0, jnp.where(even, el, before(a0 * el + d0 * after(el))))

    pl.semaphore_wait(barrier, nblocks + 2)
    to_right = pltpu.make_async_remote_copy(
        src_ref=msg_r, dst_ref=from_l, send_sem=halo_send.at[0], recv_sem=halo_recv.at[0],
        device_id=(sec, right), device_id_type=MESH,
    )
    to_left = pltpu.make_async_remote_copy(
        src_ref=msg_l, dst_ref=from_r, send_sem=halo_send.at[1], recv_sem=halo_recv.at[1],
        device_id=(sec, left), device_id_type=MESH,
    )
    to_right.start()
    to_left.start()

    top_mix = column_of(mix[0:1, :], nlev)
    top_mix = top_mix + jnp.where(rows_of((nlev, 1)) == 0, 1.0, 0.0)

    @pl.loop(0, nvar)
    def transport_substeps(v):
        acc = jnp.zeros((8, ncell), F32)
        for g in range(nlev // 8):
            span = slice(8 * g, 8 * g + 8)
            a, b, d = rate_a[span, :], rate_b[span, :], rate_d[span, :]
            x = u[v, span, :]
            for step in range(2):
                x = a * x + b * pltpu.roll(x, 1, 1) + d * pltpu.roll(x, ncell - 1, 1)
            u[v, span, :] = x
            acc = acc + top_mix[span, :] * x
        surf[pl.ds(v, 1), :] = jnp.sum(acc, axis=0, keepdims=True)

    to_right.wait()
    to_left.wait()

    fl, fr = from_l[...], from_r[...]
    rate_l, rate_r = fl[:, 2 * nvar : 2 * nvar + 1], fr[:, 2 * nvar : 2 * nvar + 1]
    add_l = jnp.where(
        even, a0 * b0 * fl + b0 * (after(fl) + rate_l * el), b1 * b0 * before(fl)
    )
    add_r = jnp.where(
        even, dm * dn * fr, an * dn * before(fr) + dn * (fr + rate_r * er)
    )
    edge_l[...] = add_l
    edge_r[...] = add_r
    wide = (nvar, LANES)
    wide_lane, wide_row = lanes_of(wide), rows_of(wide)
    for add, start, low in ((add_l, 0, 0), (add_r, ncell - LANES, LANES - 2)):
        row = jnp.broadcast_to(jnp.sum(top_mix * add, axis=0, keepdims=True), wide)
        fix = jnp.zeros(wide, F32)
        for k in range(2):
            value = jnp.sum(jnp.where(wide_lane == 2 * wide_row + k, row, 0.0), axis=1, keepdims=True)
            fix = fix + jnp.where(wide_lane == low + k, value, 0.0)
        surf[:, start : start + LANES] = surf[:, start : start + LANES] + fix

    my_group = lax.div(blk, GROUP)
    surf_pieces = pieces_of(surf[...])

    def contribution(d):
        return pltpu.make_async_remote_copy(
            src_ref=sendbuf.at[d], dst_ref=recvbuf.at[blk],
            send_sem=send_sem.at[d], recv_sem=recv_sem.at[blk],
            device_id=(other, d), device_id_type=MESH,
        )

    @pl.loop(0, ngroup)
    def pick(k):
        group = lax.rem(my_group + k, ngroup)
        chosen = picker[group] if prebuilt else selector(src, group * GROUP)
        both = jnp.dot(surf_pieces, chosen, preferred_element_type=F32)
        values = both[:nvar] + both[nvar:]
        for g in range(GROUP):
            d = group * GROUP + g
            sendbuf[d] = values[:, g * nslot : (g + 1) * nslot] * wgt[pl.ds(d, 1), :]
            contribution(d).start()

    m_high = mix[...].astype(BF16).astype(F32)
    m_low = mix[...] - m_high
    m_row = jnp.concatenate([m_high, m_low, m_high], axis=1)
    m_none = jnp.zeros_like(m_row)
    m_pair = jnp.concatenate(
        [jnp.concatenate([m_row, m_none], axis=1), jnp.concatenate([m_none, m_row], axis=1)], axis=0
    ).astype(BF16)

    @pl.loop(0, nvar // 2)
    def mix_pair(pair):
        stack, moved = [], []
        for i in range(2):
            v = 2 * pair + i
            first = u[v, :, 0:LANES] + jnp.where(lane < 2, pltpu.roll(edge_l[...], LANES - 2 * v, 1), 0.0)
            last = u[v, :, ncell - LANES : ncell] + jnp.where(
                lane >= LANES - 2, pltpu.roll(edge_r[...], LANES - 2 - 2 * v, 1), 0.0
            )
            x = jnp.concatenate([first, u[v, :, LANES : ncell - LANES], last], axis=1)
            high = x.astype(BF16).astype(F32)
            stack += [high, high, x - high]
            moved.append(x)
        mixed = jnp.dot(
            m_pair, jnp.concatenate(stack, axis=0).astype(BF16), preferred_element_type=F32
        )
        for i in range(2):
            out[0, 2 * pair + i] = moved[i] + mixed[i * nlev : (i + 1) * nlev]

    if prebuilt:

        @pl.loop(0, ngroup)
        def build_placer(g):
            placer[g] = selector(rec, g * GROUP)

    total[...] = jnp.zeros_like(total)

    @pl.loop(0, ngroup)
    def place(k):
        group = lax.rem(my_group - k + ngroup, ngroup)
        chosen = placer[group] if prebuilt else selector(rec, group * GROUP)
        values = []
        for g in range(GROUP):
            b = group * GROUP + g
            pltpu.make_async_remote_copy(
                src_ref=sendbuf.at[b], dst_ref=recvbuf.at[b],
                send_sem=send_sem.at[b], recv_sem=recv_sem.at[b],
                device_id=(other, b), device_id_type=MESH,
            ).wait_recv()
            values.append(recvbuf[b])
        total[...] += lax.dot_general(
            pieces_of(jnp.concatenate(values, axis=1)), chosen, (((1,), (1,)), ((), ())),
            preferred_element_type=F32,
        )

    arrived = total[:nvar] + total[nvar:]
    incoming[0] = arrived
    surface = surf[...]
    out[0, :, 0, :] = surface + 0.5 * (arrived - surface)

    @pl.loop(0, nblocks)
    def sent(d):
        contribution(d).wait_send()


def body(state, diffusion, transport, mixing, src_col, weights, counts, recv_rows):
    _, nvar, nlev, ncell = state.shape
    nblocks, nslot = src_col.shape[2:]
    ngroup = nblocks // GROUP
    prebuilt = nblocks * nslot * ncell * 2 <= SELECTOR_BYTES
    chosen = (ngroup, ncell, GROUP * nslot) if prebuilt else (1, 16, LANES)
    edge = pltpu.VMEM((nlev, LANES), F32)
    rate = pltpu.VMEM((nlev, ncell), F32)
    dma = pltpu.SemaphoreType.DMA
    return pl.pallas_call(
        functools.partial(kernel, nblocks, prebuilt),
        out_shape=(
            jax.ShapeDtypeStruct(state.shape, F32),
            jax.ShapeDtypeStruct((1, nvar, ncell), F32),
        ),
        in_specs=[pl.BlockSpec(memory_space=pl.ANY)] * 8,
        out_specs=[pl.BlockSpec(memory_space=pltpu.VMEM)] * 2,
        scratch_shapes=[
            pltpu.VMEM((nvar, nlev, ncell), F32),
            rate, rate,
            pltpu.VMEM((nlev, nlev), F32),
            pltpu.VMEM((nblocks, nslot), jnp.int32),
            pltpu.VMEM((nblocks, nslot), F32),
            pltpu.VMEM((1, nblocks), jnp.int32),
            pltpu.VMEM((nblocks, nslot), jnp.int32),
            rate, rate, rate,
            edge, edge, edge, edge, edge, edge,
            pltpu.VMEM((nvar, ncell), F32),
            pltpu.VMEM((nblocks, nvar, nslot), F32),
            pltpu.VMEM((nblocks, nvar, nslot), F32),
            pltpu.VMEM((2 * nvar, ncell), F32),
            pltpu.VMEM(chosen, BF16),
            pltpu.VMEM(chosen, BF16),
            dma((CHUNKS,)), dma((7,)), dma((2,)), dma((2,)),
            dma((nblocks,)), dma((nblocks,)),
        ],
        compiler_params=pltpu.CompilerParams(
            collective_id=0, has_side_effects=True, vmem_limit_bytes=40 << 20
        ),
        cost_estimate=pl.CostEstimate(
            flops=10**9, bytes_accessed=11 * 10**6, transcendentals=0
        ),
    )(state, diffusion, transport, mixing, src_col, weights, counts, recv_rows)


def solution(mesh):
    placed = (
        P("sec", None, None, "blk"),
        P("sec", None, "blk"),
        P("sec", None, "blk"),
        P("sec", None, None),
        P("sec", "blk", None, None),
        P("sec", "blk", None, None),
        P("sec", "blk", None),
        P("sec", "blk", None, None),
    )
    return jax.shard_map(
        body,
        mesh=mesh,
        in_specs=placed,
        out_specs=(P("sec", None, None, "blk"), P("sec", None, "blk")),
        check_vma=False,
    )
```

```python
import functools

import jax
import jax.numpy as jnp
from jax import lax
from jax.experimental import pallas as pl
from jax.experimental.pallas import tpu as pltpu
from jax.sharding import PartitionSpec as P

MESH = pl.DeviceIdType.MESH
F32 = jnp.float32
BF16 = jnp.bfloat16
GROUP = 2
CHUNKS = 4
LANES = 128
SELECTOR_BYTES = 8 << 20


def lanes_of(shape):
    return lax.broadcasted_iota(jnp.int32, shape, len(shape) - 1)


def rows_of(shape):
    return lax.broadcasted_iota(jnp.int32, shape, len(shape) - 2)


def column_of(row, count):
    shape = (count, row.shape[1])
    spread = jnp.where(lanes_of(shape) == rows_of(shape), jnp.broadcast_to(row, shape), 0.0)
    return jnp.sum(spread, axis=1, keepdims=True)


def pieces_of(values):
    high = values.astype(BF16)
    low = (values - high.astype(F32)).astype(BF16)
    return jnp.concatenate([high, low], axis=0)


def kernel(
    nblocks, prebuilt,
    state, diffusion, transport, mixing, src_col, weights, counts, recv_rows,
    out, incoming,
    u, dif, tra, mix, src, wgt, cnt, rec,
    rate_a, rate_b, rate_d, edge_l, edge_r, msg_l, msg_r, from_l, from_r,
    surf, sendbuf, recvbuf, total, picker, placer,
    chunk_sem, small_sem, halo_send, halo_recv, send_sem, recv_sem,
):
    nvar, nlev, ncell = u.shape
    nslot = src.shape[1]
    ngroup = nblocks // GROUP
    sec = lax.axis_index("sec")
    blk = lax.axis_index("blk")
    other = 1 - sec
    left = lax.rem(blk + nblocks - 1, nblocks)
    right = lax.rem(blk + 1, nblocks)
    barrier = pltpu.get_barrier_semaphore()

    @pl.loop(0, nblocks)
    def greet(k):
        pl.semaphore_signal(barrier, inc=1, device_id=(other, lax.rem(blk + k, nblocks)), device_id_type=MESH)

    for side in (left, right):
        pl.semaphore_signal(barrier, inc=1, device_id=(sec, side), device_id_type=MESH)

    small = [
        pltpu.make_async_copy(source, target, small_sem.at[i])
        for i, (source, target) in enumerate(
            (
                (src_col.at[0, 0], src),
                (diffusion.at[0], dif),
                (transport.at[0], tra),
                (mixing.at[0], mix),
                (weights.at[0, 0], wgt),
                (counts.at[0], cnt),
                (recv_rows.at[0, 0], rec),
            )
        )
    ]
    for copy in small:
        copy.start()
    per_chunk = nvar // CHUNKS
    chunks = [
        pltpu.make_async_copy(
            state.at[0, pl.ds(i * per_chunk, per_chunk)],
            u.at[pl.ds(i * per_chunk, per_chunk)],
            chunk_sem.at[i],
        )
        for i in range(CHUNKS)
    ]
    for copy in chunks:
        copy.start()
    for copy in small:
        copy.wait()

    def selector(index_ref, base):
        parts = []
        for g in range(GROUP):
            row = index_ref[pl.ds(base + g, 1), :]
            cells = rows_of((ncell, nslot))
            parts.append(jnp.where(cells == jnp.broadcast_to(row, (ncell, nslot)), 1.0, 0.0).astype(BF16))
        return jnp.concatenate(parts, axis=1)

    cell = lanes_of((nlev, ncell))
    d_all = dif[...]
    b_all = d_all + tra[...]
    rate_a[...] = 1.0 - d_all - b_all
    rate_b[...] = jnp.where(cell == 0, 0.0, b_all)
    rate_d[...] = jnp.where(cell == ncell - 1, 0.0, d_all)
    d_first, d_last = dif[:, :LANES], dif[:, ncell - LANES :]
    b_first = d_first + tra[:, :LANES]
    b_last = d_last + tra[:, ncell - LANES :]
    a_first, a_last = 1.0 - d_first - b_first, 1.0 - d_last - b_last
    a0, b0, b1, d0 = a_first[:, 0:1], b_first[:, 0:1], b_first[:, 1:2], d_first[:, 0:1]
    an, bn = a_last[:, LANES - 1 :], b_last[:, LANES - 1 :]
    dn, dm = d_last[:, LANES - 1 :], d_last[:, LANES - 2 : LANES - 1]

    if prebuilt:

        @pl.loop(0, ngroup)
        def build_picker(g):
            picker[g] = selector(src, g * GROUP)

    live = lanes_of(wgt.shape).astype(F32) < column_of(cnt[...].astype(F32), nblocks)
    wgt[...] = jnp.where(live, wgt[...], 0.0)

    lane = lanes_of((nlev, LANES))
    even = lax.rem(lane, 2) == 0
    edge_l[...] = jnp.zeros_like(edge_l)
    edge_r[...] = jnp.zeros_like(edge_r)
    for i in range(CHUNKS):
        chunks[i].wait()

        @pl.loop(i * per_chunk, (i + 1) * per_chunk)
        def pack(v):
            mine = lax.div(lane, 2) == v
            first = pltpu.roll(u[v, :, 0:LANES], 2 * v, 1)
            last = pltpu.roll(u[v, :, ncell - LANES : ncell], 2 * v + 2, 1)
            edge_l[...] = jnp.where(mine, first, edge_l[...])
            edge_r[...] = jnp.where(mine, last, edge_r[...])

    el, er = edge_l[...], edge_r[...]
    after = lambda x: pltpu.roll(x, LANES - 1, 1)
    before = lambda x: pltpu.roll(x, 1, 1)
    is_rate = lane == 2 * nvar
    msg_r[...] = jnp.where(is_rate, dn, jnp.where(even, after(er), an * er + bn * before(er)))
    msg_l[...] = jnp.where(is_rate, b0, jnp.where(even, el, before(a0 * el + d0 * after(el))))

    pl.semaphore_wait(barrier, nblocks + 2)
    to_right = pltpu.make_async_remote_copy(
        src_ref=msg_r, dst_ref=from_l, send_sem=halo_send.at[0], recv_sem=halo_recv.at[0],
        device_id=(sec, right), device_id_type=MESH,
    )
    to_left = pltpu.make_async_remote_copy(
        src_ref=msg_l, dst_ref=from_r, send_sem=halo_send.at[1], recv_sem=halo_recv.at[1],
        device_id=(sec, left), device_id_type=MESH,
    )
    to_right.start()
    to_left.start()

    top_mix = column_of(mix[0:1, :], nlev)
    top_mix = top_mix + jnp.where(rows_of((nlev, 1)) == 0, 1.0, 0.0)

    @pl.loop(0, nvar)
    def transport_substeps(v):
        acc = jnp.zeros((8, ncell), F32)
        for g in range(nlev // 8):
            span = slice(8 * g, 8 * g + 8)
            a, b, d = rate_a[span, :], rate_b[span, :], rate_d[span, :]
            x = u[v, span, :]
            for step in range(2):
                x = a * x + b * pltpu.roll(x, 1, 1) + d * pltpu.roll(x, ncell - 1, 1)
            u[v, span, :] = x
            acc = acc + top_mix[span, :] * x
        surf[pl.ds(v, 1), :] = jnp.sum(acc, axis=0, keepdims=True)

    to_right.wait()
    to_left.wait()

    fl, fr = from_l[...], from_r[...]
    rate_l, rate_r = fl[:, 2 * nvar : 2 * nvar + 1], fr[:, 2 * nvar : 2 * nvar + 1]
    add_l = jnp.where(
        even, a0 * b0 * fl + b0 * (after(fl) + rate_l * el), b1 * b0 * before(fl)
    )
    add_r = jnp.where(
        even, dm * dn * fr, an * dn * before(fr) + dn * (fr + rate_r * er)
    )
    edge_l[...] = add_l
    edge_r[...] = add_r
    wide = (nvar, LANES)
    wide_lane, wide_row = lanes_of(wide), rows_of(wide)
    for add, start, low in ((add_l, 0, 0), (add_r, ncell - LANES, LANES - 2)):
        row = jnp.broadcast_to(jnp.sum(top_mix * add, axis=0, keepdims=True), wide)
        fix = jnp.zeros(wide, F32)
        for k in range(2):
            value = jnp.sum(jnp.where(wide_lane == 2 * wide_row + k, row, 0.0), axis=1, keepdims=True)
            fix = fix + jnp.where(wide_lane == low + k, value, 0.0)
        surf[:, start : start + LANES] = surf[:, start : start + LANES] + fix

    my_group = lax.div(blk, GROUP)
    surf_pieces = pieces_of(surf[...])

    def contribution(d):
        return pltpu.make_async_remote_copy(
            src_ref=sendbuf.at[d], dst_ref=recvbuf.at[blk],
            send_sem=send_sem.at[d], recv_sem=recv_sem.at[blk],
            device_id=(other, d), device_id_type=MESH,
        )

    @pl.loop(0, ngroup)
    def pick(k):
        group = lax.rem(my_group + k, ngroup)
        chosen = picker[group] if prebuilt else selector(src, group * GROUP)
        both = jnp.dot(surf_pieces, chosen, preferred_element_type=F32)
        values = both[:nvar] + both[nvar:]
        for g in range(GROUP):
            d = group * GROUP + g
            sendbuf[d] = values[:, g * nslot : (g + 1) * nslot] * wgt[pl.ds(d, 1), :]
            contribution(d).start()

    m_high = mix[...].astype(BF16).astype(F32)
    m_low = mix[...] - m_high
    m_row = jnp.concatenate([m_high, m_low, m_high], axis=1)
    m_none = jnp.zeros_like(m_row)
    m_pair = jnp.concatenate(
        [jnp.concatenate([m_row, m_none], axis=1), jnp.concatenate([m_none, m_row], axis=1)], axis=0
    ).astype(BF16)

    @pl.loop(0, nvar // 2)
    def mix_pair(pair):
        stack, moved = [], []
        for i in range(2):
            v = 2 * pair + i
            first = u[v, :, 0:LANES] + jnp.where(lane < 2, pltpu.roll(edge_l[...], LANES - 2 * v, 1), 0.0)
            last = u[v, :, ncell - LANES : ncell] + jnp.where(
                lane >= LANES - 2, pltpu.roll(edge_r[...], LANES - 2 - 2 * v, 1), 0.0
            )
            x = jnp.concatenate([first, u[v, :, LANES : ncell - LANES], last], axis=1)
            high = x.astype(BF16).astype(F32)
            stack += [high, high, x - high]
            moved.append(x)
        mixed = jnp.dot(
            m_pair, jnp.concatenate(stack, axis=0).astype(BF16), preferred_element_type=F32
        )
        for i in range(2):
            out[0, 2 * pair + i] = moved[i] + mixed[i * nlev : (i + 1) * nlev]

    if prebuilt:

        @pl.loop(0, ngroup)
        def build_placer(g):
            placer[g] = selector(rec, g * GROUP)

    total[...] = jnp.zeros_like(total)

    @pl.loop(0, ngroup)
    def place(k):
        group = lax.rem(my_group - k + ngroup, ngroup)
        chosen = placer[group] if prebuilt else selector(rec, group * GROUP)
        values = []
        for g in range(GROUP):
            b = group * GROUP + g
            pltpu.make_async_remote_copy(
                src_ref=sendbuf.at[b], dst_ref=recvbuf.at[b],
                send_sem=send_sem.at[b], recv_sem=recv_sem.at[b],
                device_id=(other, b), device_id_type=MESH,
            ).wait_recv()
            values.append(recvbuf[b])
        total[...] += lax.dot_general(
            pieces_of(jnp.concatenate(values, axis=1)), chosen, (((1,), (1,)), ((), ())),
            preferred_element_type=F32,
        )

    arrived = total[:nvar] + total[nvar:]
    incoming[0] = arrived
    surface = surf[...]
    out[0, :, 0, :] = surface + 0.5 * (arrived - surface)

    @pl.loop(0, nblocks)
    def sent(d):
        contribution(d).wait_send()


def body(state, diffusion, transport, mixing, src_col, weights, counts, recv_rows):
    _, nvar, nlev, ncell = state.shape
    nblocks, nslot = src_col.shape[2:]
    ngroup = nblocks // GROUP
    prebuilt = nblocks * nslot * ncell * 2 <= SELECTOR_BYTES
    chosen = (ngroup, ncell, GROUP * nslot) if prebuilt else (1, 16, LANES)
    edge = pltpu.VMEM((nlev, LANES), F32)
    rate = pltpu.VMEM((nlev, ncell), F32)
    dma = pltpu.SemaphoreType.DMA
    inputs = [
        pltpu.with_memory_space_constraint(x, pltpu.HBM)
        for x in (state, diffusion, transport, mixing, src_col, weights, counts, recv_rows)
    ]
    return pl.pallas_call(
        functools.partial(kernel, nblocks, prebuilt),
        out_shape=(
            jax.ShapeDtypeStruct(state.shape, F32),
            jax.ShapeDtypeStruct((1, nvar, ncell), F32),
        ),
        in_specs=[pl.BlockSpec(memory_space=pltpu.HBM)] * 8,
        out_specs=[pl.BlockSpec(memory_space=pltpu.VMEM)] * 2,
        scratch_shapes=[
            pltpu.VMEM((nvar, nlev, ncell), F32),
            rate, rate,
            pltpu.VMEM((nlev, nlev), F32),
            pltpu.VMEM((nblocks, nslot), jnp.int32),
            pltpu.VMEM((nblocks, nslot), F32),
            pltpu.VMEM((1, nblocks), jnp.int32),
            pltpu.VMEM((nblocks, nslot), jnp.int32),
            rate, rate, rate,
            edge, edge, edge, edge, edge, edge,
            pltpu.VMEM((nvar, ncell), F32),
            pltpu.VMEM((nblocks, nvar, nslot), F32),
            pltpu.VMEM((nblocks, nvar, nslot), F32),
            pltpu.VMEM((2 * nvar, ncell), F32),
            pltpu.VMEM(chosen, BF16),
            pltpu.VMEM(chosen, BF16),
            dma((CHUNKS,)), dma((7,)), dma((2,)), dma((2,)),
            dma((nblocks,)), dma((nblocks,)),
        ],
        compiler_params=pltpu.CompilerParams(
            collective_id=0, has_side_effects=True, vmem_limit_bytes=40 << 20
        ),
        cost_estimate=pl.CostEstimate(
            flops=10**9, bytes_accessed=11 * 10**6, transcendentals=0
        ),
    )(*inputs)


def solution(mesh):
    placed = (
        P("sec", None, None, "blk"),
        P("sec", None, "blk"),
        P("sec", None, "blk"),
        P("sec", None, None),
        P("sec", "blk", None, None),
        P("sec", "blk", None, None),
        P("sec", "blk", None),
        P("sec", "blk", None, None),
    )
    return jax.shard_map(
        body,
        mesh=mesh,
        in_specs=placed,
        out_specs=(P("sec", None, None, "blk"), P("sec", None, "blk")),
        check_vma=False,
    )
```

```python
import functools

import jax
import jax.numpy as jnp
from jax import lax
from jax.experimental import pallas as pl
from jax.experimental.pallas import tpu as pltpu
from jax.sharding import PartitionSpec as P

MESH = pl.DeviceIdType.MESH
F32 = jnp.float32
BF16 = jnp.bfloat16
GROUP = 4
UNROLL = 1
CHUNKS = 4
LANES = 128
SELECTOR_BYTES = 8 << 20


def lanes_of(shape):
    return lax.broadcasted_iota(jnp.int32, shape, len(shape) - 1)


def rows_of(shape):
    return lax.broadcasted_iota(jnp.int32, shape, len(shape) - 2)


def column_of(row, count):
    shape = (count, row.shape[1])
    spread = jnp.where(lanes_of(shape) == rows_of(shape), jnp.broadcast_to(row, shape), 0.0)
    return jnp.sum(spread, axis=1, keepdims=True)


def pieces_of(values):
    high = values.astype(BF16)
    low = (values - high.astype(F32)).astype(BF16)
    return jnp.concatenate([high, low], axis=0)


def kernel(
    nblocks, prebuilt,
    state, diffusion, transport, mixing, src_col, weights, counts, recv_rows,
    out, incoming,
    u, dif, tra, mix, src, wgt, cnt, rec,
    coef, level_mix, edge_l, edge_r, msg_l, msg_r, from_l, from_r,
    surf, sendbuf, recvbuf, total, picker, placer,
    chunk_sem, small_sem, halo_send, halo_recv, send_sem, recv_sem,
):
    nvar, nlev, ncell = u.shape
    nslot = src.shape[1]
    ngroup = nblocks // GROUP
    sec = lax.axis_index("sec")
    blk = lax.axis_index("blk")
    other = 1 - sec
    left = lax.rem(blk + nblocks - 1, nblocks)
    right = lax.rem(blk + 1, nblocks)
    barrier = pltpu.get_barrier_semaphore()

    @pl.loop(0, nblocks)
    def greet(k):
        pl.semaphore_signal(barrier, inc=1, device_id=(other, lax.rem(blk + k, nblocks)), device_id_type=MESH)

    for side in (left, right):
        pl.semaphore_signal(barrier, inc=1, device_id=(sec, side), device_id_type=MESH)

    small = [
        pltpu.make_async_copy(source, target, small_sem.at[i])
        for i, (source, target) in enumerate(
            (
                (src_col.at[0, 0], src),
                (diffusion.at[0], dif),
                (transport.at[0], tra),
                (mixing.at[0], mix),
                (weights.at[0, 0], wgt),
                (counts.at[0], cnt),
                (recv_rows.at[0, 0], rec),
            )
        )
    ]
    for copy in small:
        copy.start()
    per_chunk = nvar // CHUNKS
    chunks = [
        pltpu.make_async_copy(
            state.at[0, pl.ds(i * per_chunk, per_chunk)],
            u.at[pl.ds(i * per_chunk, per_chunk)],
            chunk_sem.at[i],
        )
        for i in range(CHUNKS)
    ]
    for copy in chunks:
        copy.start()
    for copy in small:
        copy.wait()

    def selector(index_ref, base):
        parts = []
        for g in range(GROUP):
            row = index_ref[pl.ds(base + g, 1), :]
            cells = rows_of((ncell, nslot))
            parts.append(jnp.where(cells == jnp.broadcast_to(row, (ncell, nslot)), 1.0, 0.0).astype(BF16))
        return jnp.concatenate(parts, axis=1)

    cell = lanes_of((nlev, ncell))
    d_all = dif[...]
    b_all = d_all + tra[...]
    a_all = 1.0 - d_all - b_all
    b_in = jnp.where(cell == 0, 0.0, b_all)
    d_in = jnp.where(cell == ncell - 1, 0.0, d_all)
    coef[0] = b_in * pltpu.roll(b_in, 1, 1)
    coef[1] = b_in * (a_all + pltpu.roll(a_all, 1, 1))
    coef[2] = a_all * a_all + b_in * pltpu.roll(d_in, 1, 1) + d_in * pltpu.roll(b_in, ncell - 1, 1)
    coef[3] = d_in * (a_all + pltpu.roll(a_all, ncell - 1, 1))
    coef[4] = d_in * pltpu.roll(d_in, ncell - 1, 1)
    d_first, d_last = dif[:, :LANES], dif[:, ncell - LANES :]
    b_first = d_first + tra[:, :LANES]
    b_last = d_last + tra[:, ncell - LANES :]
    a_first, a_last = 1.0 - d_first - b_first, 1.0 - d_last - b_last
    a0, b0, b1, d0 = a_first[:, 0:1], b_first[:, 0:1], b_first[:, 1:2], d_first[:, 0:1]
    an, bn = a_last[:, LANES - 1 :], b_last[:, LANES - 1 :]
    dn, dm = d_last[:, LANES - 1 :], d_last[:, LANES - 2 : LANES - 1]

    if prebuilt:

        @pl.loop(0, ngroup)
        def build_picker(g):
            picker[g] = selector(src, g * GROUP)

    live = lanes_of(wgt.shape).astype(F32) < column_of(cnt[...].astype(F32), nblocks)
    wgt[...] = jnp.where(live, wgt[...], 0.0)

    lane = lanes_of((nlev, LANES))
    even = lax.rem(lane, 2) == 0
    edge_l[...] = jnp.zeros_like(edge_l)
    edge_r[...] = jnp.zeros_like(edge_r)
    for i in range(CHUNKS):
        chunks[i].wait()

        @pl.loop(i * per_chunk, (i + 1) * per_chunk)
        def pack(v):
            mine = lax.div(lane, 2) == v
            first = pltpu.roll(u[v, :, 0:LANES], 2 * v, 1)
            last = pltpu.roll(u[v, :, ncell - LANES : ncell], 2 * v + 2, 1)
            edge_l[...] = jnp.where(mine, first, edge_l[...])
            edge_r[...] = jnp.where(mine, last, edge_r[...])

    el, er = edge_l[...], edge_r[...]
    after = lambda x: pltpu.roll(x, LANES - 1, 1)
    before = lambda x: pltpu.roll(x, 1, 1)
    is_rate = lane == 2 * nvar
    msg_r[...] = jnp.where(is_rate, dn, jnp.where(even, after(er), an * er + bn * before(er)))
    msg_l[...] = jnp.where(is_rate, b0, jnp.where(even, el, before(a0 * el + d0 * after(el))))

    pl.semaphore_wait(barrier, nblocks + 2)
    to_right = pltpu.make_async_remote_copy(
        src_ref=msg_r, dst_ref=from_l, send_sem=halo_send.at[0], recv_sem=halo_recv.at[0],
        device_id=(sec, right), device_id_type=MESH,
    )
    to_left = pltpu.make_async_remote_copy(
        src_ref=msg_l, dst_ref=from_r, send_sem=halo_send.at[1], recv_sem=halo_recv.at[1],
        device_id=(sec, left), device_id_type=MESH,
    )
    to_right.start()
    to_left.start()

    top_mix = column_of(mix[0:1, :], nlev)
    top_mix = top_mix + jnp.where(rows_of((nlev, 1)) == 0, 1.0, 0.0)

    level_mix[...] = jnp.broadcast_to(top_mix, level_mix.shape)

    @pl.loop(0, nvar, unroll=UNROLL)
    def transport_substeps(v):
        acc = jnp.zeros((8, ncell), F32)
        for g in range(nlev // 8):
            span = slice(8 * g, 8 * g + 8)
            old = u[v, span, :]
            x = coef[2, span, :] * old
            for k, shift in enumerate((2, 1, 0, ncell - 1, ncell - 2)):
                if shift:
                    x = x + coef[k, span, :] * pltpu.roll(old, shift, 1)
            u[v, span, :] = x
            scale = level_mix[span, :]
            acc = acc + jnp.concatenate([scale] * (ncell // LANES), axis=1) * x
        surf[pl.ds(v, 1), :] = jnp.sum(acc, axis=0, keepdims=True)

    to_right.wait()
    to_left.wait()

    fl, fr = from_l[...], from_r[...]
    rate_l, rate_r = fl[:, 2 * nvar : 2 * nvar + 1], fr[:, 2 * nvar : 2 * nvar + 1]
    add_l = jnp.where(
        even, a0 * b0 * fl + b0 * (after(fl) + rate_l * el), b1 * b0 * before(fl)
    )
    add_r = jnp.where(
        even, dm * dn * fr, an * dn * before(fr) + dn * (fr + rate_r * er)
    )
    edge_l[...] = add_l
    edge_r[...] = add_r
    wide = (nvar, LANES)
    wide_lane, wide_row = lanes_of(wide), rows_of(wide)
    for add, start, low in ((add_l, 0, 0), (add_r, ncell - LANES, LANES - 2)):
        row = jnp.broadcast_to(jnp.sum(top_mix * add, axis=0, keepdims=True), wide)
        fix = jnp.zeros(wide, F32)
        for k in range(2):
            value = jnp.sum(jnp.where(wide_lane == 2 * wide_row + k, row, 0.0), axis=1, keepdims=True)
            fix = fix + jnp.where(wide_lane == low + k, value, 0.0)
        surf[:, start : start + LANES] = surf[:, start : start + LANES] + fix

    my_group = lax.div(blk, GROUP)
    surf_pieces = pieces_of(surf[...])

    def contribution(d):
        return pltpu.make_async_remote_copy(
            src_ref=sendbuf.at[d], dst_ref=recvbuf.at[blk],
            send_sem=send_sem.at[d], recv_sem=recv_sem.at[blk],
            device_id=(other, d), device_id_type=MESH,
        )

    @pl.loop(0, ngroup)
    def pick(k):
        group = lax.rem(my_group + k, ngroup)
        chosen = picker[group] if prebuilt else selector(src, group * GROUP)
        both = jnp.dot(surf_pieces, chosen, preferred_element_type=F32)
        values = both[:nvar] + both[nvar:]
        for g in range(GROUP):
            d = group * GROUP + g
            sendbuf[d] = values[:, g * nslot : (g + 1) * nslot] * wgt[pl.ds(d, 1), :]
            contribution(d).start()

    m_high = mix[...].astype(BF16).astype(F32)
    m_low = mix[...] - m_high
    m_row = jnp.concatenate([m_high, m_low, m_high], axis=1)
    m_none = jnp.zeros_like(m_row)
    m_pair = jnp.concatenate(
        [jnp.concatenate([m_row, m_none], axis=1), jnp.concatenate([m_none, m_row], axis=1)], axis=0
    ).astype(BF16)

    @pl.loop(0, nvar // 2)
    def mix_pair(pair):
        stack, moved = [], []
        for i in range(2):
            v = 2 * pair + i
            first = u[v, :, 0:LANES] + jnp.where(lane < 2, pltpu.roll(edge_l[...], LANES - 2 * v, 1), 0.0)
            last = u[v, :, ncell - LANES : ncell] + jnp.where(
                lane >= LANES - 2, pltpu.roll(edge_r[...], LANES - 2 - 2 * v, 1), 0.0
            )
            x = jnp.concatenate([first, u[v, :, LANES : ncell - LANES], last], axis=1)
            high = x.astype(BF16).astype(F32)
            stack += [high, high, x - high]
            moved.append(x)
        mixed = jnp.dot(
            m_pair, jnp.concatenate(stack, axis=0).astype(BF16), preferred_element_type=F32
        )
        for i in range(2):
            out[0, 2 * pair + i] = moved[i] + mixed[i * nlev : (i + 1) * nlev]

    if prebuilt:

        @pl.loop(0, ngroup)
        def build_placer(g):
            placer[g] = selector(rec, g * GROUP)

    total[...] = jnp.zeros_like(total)

    @pl.loop(0, ngroup)
    def place(k):
        group = lax.rem(my_group - k + ngroup, ngroup)
        chosen = placer[group] if prebuilt else selector(rec, group * GROUP)
        values = []
        for g in range(GROUP):
            b = group * GROUP + g
            pltpu.make_async_remote_copy(
                src_ref=sendbuf.at[b], dst_ref=recvbuf.at[b],
                send_sem=send_sem.at[b], recv_sem=recv_sem.at[b],
                device_id=(other, b), device_id_type=MESH,
            ).wait_recv()
            values.append(recvbuf[b])
        total[...] += lax.dot_general(
            pieces_of(jnp.concatenate(values, axis=1)), chosen, (((1,), (1,)), ((), ())),
            preferred_element_type=F32,
        )

    arrived = total[:nvar] + total[nvar:]
    incoming[0] = arrived
    surface = surf[...]
    out[0, :, 0, :] = surface + 0.5 * (arrived - surface)

    @pl.loop(0, nblocks)
    def sent(d):
        contribution(d).wait_send()


def write_out(column, arrived, new_state, incoming, sems):
    per = column.shape[1] // CHUNKS
    copies = [
        pltpu.make_async_copy(
            column.at[0, pl.ds(i * per, per)], new_state.at[0, pl.ds(i * per, per)], sems.at[i]
        )
        for i in range(CHUNKS)
    ]
    copies.append(pltpu.make_async_copy(arrived, incoming, sems.at[CHUNKS]))
    for copy in copies:
        copy.start()
    for copy in copies:
        copy.wait()


def body(state, diffusion, transport, mixing, src_col, weights, counts, recv_rows):
    _, nvar, nlev, ncell = state.shape
    nblocks, nslot = src_col.shape[2:]
    ngroup = nblocks // GROUP
    prebuilt = nblocks * nslot * ncell * 2 <= SELECTOR_BYTES
    chosen = (ngroup, ncell, GROUP * nslot) if prebuilt else (1, 16, LANES)
    edge = pltpu.VMEM((nlev, LANES), F32)
    rate = pltpu.VMEM((nlev, ncell), F32)
    dma = pltpu.SemaphoreType.DMA
    inputs = [
        pltpu.with_memory_space_constraint(x, pltpu.HBM)
        for x in (state, diffusion, transport, mixing, src_col, weights, counts, recv_rows)
    ]
    shapes = (
        jax.ShapeDtypeStruct(state.shape, F32),
        jax.ShapeDtypeStruct((1, nvar, ncell), F32),
    )
    column, arrived = pl.pallas_call(
        functools.partial(kernel, nblocks, prebuilt),
        out_shape=shapes,
        in_specs=[pl.BlockSpec(memory_space=pltpu.HBM)] * 8,
        out_specs=[pl.BlockSpec(memory_space=pltpu.VMEM)] * 2,
        scratch_shapes=[
            pltpu.VMEM((nvar, nlev, ncell), F32),
            rate, rate,
            pltpu.VMEM((nlev, nlev), F32),
            pltpu.VMEM((nblocks, nslot), jnp.int32),
            pltpu.VMEM((nblocks, nslot), F32),
            pltpu.VMEM((1, nblocks), jnp.int32),
            pltpu.VMEM((nblocks, nslot), jnp.int32),
            pltpu.VMEM((5, nlev, ncell), F32),
            edge, edge, edge, edge, edge, edge, edge,
            pltpu.VMEM((nvar, ncell), F32),
            pltpu.VMEM((nblocks, nvar, nslot), F32),
            pltpu.VMEM((nblocks, nvar, nslot), F32),
            pltpu.VMEM((2 * nvar, ncell), F32),
            pltpu.VMEM(chosen, BF16),
            pltpu.VMEM(chosen, BF16),
            dma((CHUNKS,)), dma((7,)), dma((2,)), dma((2,)),
            dma((nblocks,)), dma((nblocks,)),
        ],
        compiler_params=pltpu.CompilerParams(
            collective_id=0, has_side_effects=True, vmem_limit_bytes=40 << 20
        ),
        cost_estimate=pl.CostEstimate(
            flops=10**9, bytes_accessed=11 * 10**6, transcendentals=0
        ),
    )(*inputs)
    return tuple(
        pl.pallas_call(
            write_out,
            out_shape=shapes,
            in_specs=[pl.BlockSpec(memory_space=pl.ANY)] * 2,
            out_specs=[pl.BlockSpec(memory_space=pl.ANY)] * 2,
            scratch_shapes=[dma((CHUNKS + 1,))],
            compiler_params=pltpu.CompilerParams(vmem_limit_bytes=40 << 20),
        )(column, arrived)
    )


def solution(mesh):
    placed = (
        P("sec", None, None, "blk"),
        P("sec", None, "blk"),
        P("sec", None, "blk"),
        P("sec", None, None),
        P("sec", "blk", None, None),
        P("sec", "blk", None, None),
        P("sec", "blk", None),
        P("sec", "blk", None, None),
    )
    return jax.shard_map(
        body,
        mesh=mesh,
        in_specs=placed,
        out_specs=(P("sec", None, None, "blk"), P("sec", None, "blk")),
        check_vma=False,
    )
```

```python
import functools

import jax
import jax.numpy as jnp
from jax import lax
from jax.experimental import pallas as pl
from jax.experimental.pallas import tpu as pltpu
from jax.sharding import PartitionSpec as P

MESH = pl.DeviceIdType.MESH
F32 = jnp.float32
BF16 = jnp.bfloat16
GROUP = 4
CHUNKS = 4
LANES = 128
SELECTOR_BYTES = 8 << 20


def lanes_of(shape):
    return lax.broadcasted_iota(jnp.int32, shape, len(shape) - 1)


def rows_of(shape):
    return lax.broadcasted_iota(jnp.int32, shape, len(shape) - 2)


def column_of(row, count):
    shape = (count, row.shape[1])
    spread = jnp.where(lanes_of(shape) == rows_of(shape), jnp.broadcast_to(row, shape), 0.0)
    return jnp.sum(spread, axis=1, keepdims=True)


def pieces_of(values):
    high = values.astype(BF16)
    low = (values - high.astype(F32)).astype(BF16)
    return jnp.concatenate([high, low], axis=0)


def kernel(
    nblocks, prebuilt,
    state, diffusion, transport, mixing, src_col, weights, counts, recv_rows,
    out, incoming,
    u, dif, tra, mix, src, wgt, cnt, rec,
    coef, level_mix, edge_l, edge_r, msg_l, msg_r, from_l, from_r,
    surf, sendbuf, recvbuf, total, picker, placer,
    chunk_sem, small_sem, halo_send, halo_recv, send_sem, recv_sem,
):
    nvar, nlev, ncell = u.shape
    nslot = src.shape[1]
    ngroup = nblocks // GROUP
    sec = lax.axis_index("sec")
    blk = lax.axis_index("blk")
    other = 1 - sec
    left = lax.rem(blk + nblocks - 1, nblocks)
    right = lax.rem(blk + 1, nblocks)
    barrier = pltpu.get_barrier_semaphore()

    @pl.loop(0, nblocks)
    def greet(k):
        pl.semaphore_signal(barrier, inc=1, device_id=(other, lax.rem(blk + k, nblocks)), device_id_type=MESH)

    for side in (left, right):
        pl.semaphore_signal(barrier, inc=1, device_id=(sec, side), device_id_type=MESH)

    small = [
        pltpu.make_async_copy(source, target, small_sem.at[i])
        for i, (source, target) in enumerate(
            (
                (src_col.at[0, 0], src),
                (diffusion.at[0], dif),
                (transport.at[0], tra),
                (mixing.at[0], mix),
                (weights.at[0, 0], wgt),
                (counts.at[0], cnt),
                (recv_rows.at[0, 0], rec),
            )
        )
    ]
    for copy in small:
        copy.start()
    per_chunk = nvar // CHUNKS
    chunks = [
        pltpu.make_async_copy(
            state.at[0, pl.ds(i * per_chunk, per_chunk)],
            u.at[pl.ds(i * per_chunk, per_chunk)],
            chunk_sem.at[i],
        )
        for i in range(CHUNKS)
    ]
    for copy in chunks:
        copy.start()
    for copy in small:
        copy.wait()

    def selector(index_ref, base):
        parts = []
        for g in range(GROUP):
            row = index_ref[pl.ds(base + g, 1), :]
            cells = rows_of((ncell, nslot))
            parts.append(jnp.where(cells == jnp.broadcast_to(row, (ncell, nslot)), 1.0, 0.0).astype(BF16))
        return jnp.concatenate(parts, axis=1)

    cell = lanes_of((nlev, ncell))
    d_all = dif[...]
    b_all = d_all + tra[...]
    a_all = 1.0 - d_all - b_all
    b_in = jnp.where(cell == 0, 0.0, b_all)
    d_in = jnp.where(cell == ncell - 1, 0.0, d_all)
    coef[0] = b_in * pltpu.roll(b_in, 1, 1)
    coef[1] = b_in * (a_all + pltpu.roll(a_all, 1, 1))
    coef[2] = a_all * a_all + b_in * pltpu.roll(d_in, 1, 1) + d_in * pltpu.roll(b_in, ncell - 1, 1)
    coef[3] = d_in * (a_all + pltpu.roll(a_all, ncell - 1, 1))
    coef[4] = d_in * pltpu.roll(d_in, ncell - 1, 1)
    d_first, d_last = dif[:, :LANES], dif[:, ncell - LANES :]
    b_first = d_first + tra[:, :LANES]
    b_last = d_last + tra[:, ncell - LANES :]
    a_first, a_last = 1.0 - d_first - b_first, 1.0 - d_last - b_last
    a0, b0, b1, d0 = a_first[:, 0:1], b_first[:, 0:1], b_first[:, 1:2], d_first[:, 0:1]
    an, bn = a_last[:, LANES - 1 :], b_last[:, LANES - 1 :]
    dn, dm = d_last[:, LANES - 1 :], d_last[:, LANES - 2 : LANES - 1]

    if prebuilt:

        @pl.loop(0, ngroup)
        def build_picker(g):
            picker[g] = selector(src, g * GROUP)

    live = lanes_of(wgt.shape).astype(F32) < column_of(cnt[...].astype(F32), nblocks)
    wgt[...] = jnp.where(live, wgt[...], 0.0)

    lane = lanes_of((nlev, LANES))
    even = lax.rem(lane, 2) == 0
    edge_l[...] = jnp.zeros_like(edge_l)
    edge_r[...] = jnp.zeros_like(edge_r)
    for i in range(CHUNKS):
        chunks[i].wait()

        @pl.loop(i * per_chunk, (i + 1) * per_chunk)
        def pack(v):
            mine = lax.div(lane, 2) == v
            first = pltpu.roll(u[v, :, 0:LANES], 2 * v, 1)
            last = pltpu.roll(u[v, :, ncell - LANES : ncell], 2 * v + 2, 1)
            edge_l[...] = jnp.where(mine, first, edge_l[...])
            edge_r[...] = jnp.where(mine, last, edge_r[...])

    el, er = edge_l[...], edge_r[...]
    after = lambda x: pltpu.roll(x, LANES - 1, 1)
    before = lambda x: pltpu.roll(x, 1, 1)
    is_rate = lane == 2 * nvar
    msg_r[...] = jnp.where(is_rate, dn, jnp.where(even, after(er), an * er + bn * before(er)))
    msg_l[...] = jnp.where(is_rate, b0, jnp.where(even, el, before(a0 * el + d0 * after(el))))

    pl.semaphore_wait(barrier, nblocks + 2)
    to_right = pltpu.make_async_remote_copy(
        src_ref=msg_r, dst_ref=from_l, send_sem=halo_send.at[0], recv_sem=halo_recv.at[0],
        device_id=(sec, right), device_id_type=MESH,
    )
    to_left = pltpu.make_async_remote_copy(
        src_ref=msg_l, dst_ref=from_r, send_sem=halo_send.at[1], recv_sem=halo_recv.at[1],
        device_id=(sec, left), device_id_type=MESH,
    )
    to_right.start()
    to_left.start()

    top_mix = column_of(mix[0:1, :], nlev)
    top_mix = top_mix + jnp.where(rows_of((nlev, 1)) == 0, 1.0, 0.0)

    level_mix[...] = jnp.broadcast_to(top_mix, level_mix.shape)

    count = ncell // LANES

    @pl.loop(0, nvar // 2)
    def transport_substeps(pair):
        acc = [[jnp.zeros((8, LANES), F32)] * count for _ in range(2)]
        for g in range(nlev // 8):
            span = slice(8 * g, 8 * g + 8)
            scale = level_mix[span, :]
            old = [u[2 * pair + w, span, :] for w in range(2)]
            turned = [
                {
                    shift: pltpu.roll(x, shift % ncell, 1)
                    for shift in (2, 1, -1, -2)
                }
                for x in old
            ]
            new = [[], []]
            for i in range(count):
                at = slice(i * LANES, (i + 1) * LANES)
                rates = [coef[k, span, at] for k in range(5)]
                for w in range(2):
                    y = rates[2] * old[w][:, at]
                    for k, shift in ((0, 2), (1, 1), (3, -1), (4, -2)):
                        y = y + rates[k] * turned[w][shift][:, at]
                    new[w].append(y)
                    acc[w][i] = acc[w][i] + scale * y
            for w in range(2):
                u[2 * pair + w, span, :] = jnp.concatenate(new[w], axis=1)
        for w in range(2):
            surf[pl.ds(2 * pair + w, 1), :] = jnp.sum(
                jnp.concatenate(acc[w], axis=1), axis=0, keepdims=True
            )

    to_right.wait()
    to_left.wait()

    fl, fr = from_l[...], from_r[...]
    rate_l, rate_r = fl[:, 2 * nvar : 2 * nvar + 1], fr[:, 2 * nvar : 2 * nvar + 1]
    add_l = jnp.where(
        even, a0 * b0 * fl + b0 * (after(fl) + rate_l * el), b1 * b0 * before(fl)
    )
    add_r = jnp.where(
        even, dm * dn * fr, an * dn * before(fr) + dn * (fr + rate_r * er)
    )
    edge_l[...] = add_l
    edge_r[...] = add_r
    wide = (nvar, LANES)
    wide_lane, wide_row = lanes_of(wide), rows_of(wide)
    for add, start, low in ((add_l, 0, 0), (add_r, ncell - LANES, LANES - 2)):
        row = jnp.broadcast_to(jnp.sum(top_mix * add, axis=0, keepdims=True), wide)
        fix = jnp.zeros(wide, F32)
        for k in range(2):
            value = jnp.sum(jnp.where(wide_lane == 2 * wide_row + k, row, 0.0), axis=1, keepdims=True)
            fix = fix + jnp.where(wide_lane == low + k, value, 0.0)
        surf[:, start : start + LANES] = surf[:, start : start + LANES] + fix

    my_group = lax.div(blk, GROUP)
    surf_pieces = pieces_of(surf[...])

    def contribution(d):
        return pltpu.make_async_remote_copy(
            src_ref=sendbuf.at[d], dst_ref=recvbuf.at[blk],
            send_sem=send_sem.at[d], recv_sem=recv_sem.at[blk],
            device_id=(other, d), device_id_type=MESH,
        )

    @pl.loop(0, ngroup)
    def pick(k):
        group = lax.rem(my_group + k, ngroup)
        chosen = picker[group] if prebuilt else selector(src, group * GROUP)
        both = jnp.dot(surf_pieces, chosen, preferred_element_type=F32)
        values = both[:nvar] + both[nvar:]
        for g in range(GROUP):
            d = group * GROUP + g
            sendbuf[d] = values[:, g * nslot : (g + 1) * nslot] * wgt[pl.ds(d, 1), :]
            contribution(d).start()

    m_high = mix[...].astype(BF16).astype(F32)
    m_low = mix[...] - m_high
    m_row = jnp.concatenate([m_high, m_low, m_high], axis=1)
    m_none = jnp.zeros_like(m_row)
    m_pair = jnp.concatenate(
        [jnp.concatenate([m_row, m_none], axis=1), jnp.concatenate([m_none, m_row], axis=1)], axis=0
    ).astype(BF16)

    @pl.loop(0, nvar // 2)
    def mix_pair(pair):
        stack, moved = [], []
        for i in range(2):
            v = 2 * pair + i
            first = u[v, :, 0:LANES] + jnp.where(lane < 2, pltpu.roll(edge_l[...], LANES - 2 * v, 1), 0.0)
            last = u[v, :, ncell - LANES : ncell] + jnp.where(
                lane >= LANES - 2, pltpu.roll(edge_r[...], LANES - 2 - 2 * v, 1), 0.0
            )
            x = jnp.concatenate([first, u[v, :, LANES : ncell - LANES], last], axis=1)
            high = x.astype(BF16).astype(F32)
            stack += [high, high, x - high]
            moved.append(x)
        mixed = jnp.dot(
            m_pair, jnp.concatenate(stack, axis=0).astype(BF16), preferred_element_type=F32
        )
        for i in range(2):
            out[0, 2 * pair + i] = moved[i] + mixed[i * nlev : (i + 1) * nlev]

    if prebuilt:

        @pl.loop(0, ngroup)
        def build_placer(g):
            placer[g] = selector(rec, g * GROUP)

    total[...] = jnp.zeros_like(total)

    @pl.loop(0, ngroup)
    def place(k):
        group = lax.rem(my_group - k + ngroup, ngroup)
        chosen = placer[group] if prebuilt else selector(rec, group * GROUP)
        values = []
        for g in range(GROUP):
            b = group * GROUP + g
            pltpu.make_async_remote_copy(
                src_ref=sendbuf.at[b], dst_ref=recvbuf.at[b],
                send_sem=send_sem.at[b], recv_sem=recv_sem.at[b],
                device_id=(other, b), device_id_type=MESH,
            ).wait_recv()
            values.append(recvbuf[b])
        total[...] += lax.dot_general(
            pieces_of(jnp.concatenate(values, axis=1)), chosen, (((1,), (1,)), ((), ())),
            preferred_element_type=F32,
        )

    arrived = total[:nvar] + total[nvar:]
    incoming[0] = arrived
    surface = surf[...]
    out[0, :, 0, :] = surface + 0.5 * (arrived - surface)

    @pl.loop(0, nblocks)
    def sent(d):
        contribution(d).wait_send()


def write_out(column, arrived, new_state, incoming, sems):
    per = column.shape[1] // CHUNKS
    copies = [
        pltpu.make_async_copy(
            column.at[0, pl.ds(i * per, per)], new_state.at[0, pl.ds(i * per, per)], sems.at[i]
        )
        for i in range(CHUNKS)
    ]
    copies.append(pltpu.make_async_copy(arrived, incoming, sems.at[CHUNKS]))
    for copy in copies:
        copy.start()
    for copy in copies:
        copy.wait()


def body(state, diffusion, transport, mixing, src_col, weights, counts, recv_rows):
    _, nvar, nlev, ncell = state.shape
    nblocks, nslot = src_col.shape[2:]
    ngroup = nblocks // GROUP
    prebuilt = nblocks * nslot * ncell * 2 <= SELECTOR_BYTES
    chosen = (ngroup, ncell, GROUP * nslot) if prebuilt else (1, 16, LANES)
    edge = pltpu.VMEM((nlev, LANES), F32)
    rate = pltpu.VMEM((nlev, ncell), F32)
    dma = pltpu.SemaphoreType.DMA
    inputs = [
        pltpu.with_memory_space_constraint(x, pltpu.HBM)
        for x in (state, diffusion, transport, mixing, src_col, weights, counts, recv_rows)
    ]
    shapes = (
        jax.ShapeDtypeStruct(state.shape, F32),
        jax.ShapeDtypeStruct((1, nvar, ncell), F32),
    )
    column, arrived = pl.pallas_call(
        functools.partial(kernel, nblocks, prebuilt),
        out_shape=shapes,
        in_specs=[pl.BlockSpec(memory_space=pltpu.HBM)] * 8,
        out_specs=[pl.BlockSpec(memory_space=pltpu.VMEM)] * 2,
        scratch_shapes=[
            pltpu.VMEM((nvar, nlev, ncell), F32),
            rate, rate,
            pltpu.VMEM((nlev, nlev), F32),
            pltpu.VMEM((nblocks, nslot), jnp.int32),
            pltpu.VMEM((nblocks, nslot), F32),
            pltpu.VMEM((1, nblocks), jnp.int32),
            pltpu.VMEM((nblocks, nslot), jnp.int32),
            pltpu.VMEM((5, nlev, ncell), F32),
            edge, edge, edge, edge, edge, edge, edge,
            pltpu.VMEM((nvar, ncell), F32),
            pltpu.VMEM((nblocks, nvar, nslot), F32),
            pltpu.VMEM((nblocks, nvar, nslot), F32),
            pltpu.VMEM((2 * nvar, ncell), F32),
            pltpu.VMEM(chosen, BF16),
            pltpu.VMEM(chosen, BF16),
            dma((CHUNKS,)), dma((7,)), dma((2,)), dma((2,)),
            dma((nblocks,)), dma((nblocks,)),
        ],
        compiler_params=pltpu.CompilerParams(
            collective_id=0, has_side_effects=True, vmem_limit_bytes=40 << 20
        ),
        cost_estimate=pl.CostEstimate(
            flops=10**9, bytes_accessed=11 * 10**6, transcendentals=0
        ),
    )(*inputs)
    return tuple(
        pl.pallas_call(
            write_out,
            out_shape=shapes,
            in_specs=[pl.BlockSpec(memory_space=pl.ANY)] * 2,
            out_specs=[pl.BlockSpec(memory_space=pl.ANY)] * 2,
            scratch_shapes=[dma((CHUNKS + 1,))],
            compiler_params=pltpu.CompilerParams(vmem_limit_bytes=40 << 20),
        )(column, arrived)
    )


def solution(mesh):
    placed = (
        P("sec", None, None, "blk"),
        P("sec", None, "blk"),
        P("sec", None, "blk"),
        P("sec", None, None),
        P("sec", "blk", None, None),
        P("sec", "blk", None, None),
        P("sec", "blk", None),
        P("sec", "blk", None, None),
    )
    return jax.shard_map(
        body,
        mesh=mesh,
        in_specs=placed,
        out_specs=(P("sec", None, None, "blk"), P("sec", None, "blk")),
        check_vma=False,
    )
```
